256 devices in a mesh: dp: 32 (over x, z_hi, core), ctx: 8 (over y, z_lo).
Axes of the slice: x: 4, y: 4, z: 8 (z_hi: 4, z_lo: 2; z = z_hi * 2 + z_lo), core: 2. Of those that a mesh axis runs over, the one named last changes fastest.
Arguments:
- queries: bfloat16 [131072, 1024], P(('dp', 'ctx')), may hold values from -6 to 6
- keys_values: bfloat16 [131072, 1, 2, 128], P(('dp', 'ctx')), may hold values from -6 to 6
- routing: int32 [131072, 2], P(('dp', 'ctx')), may hold values from 0 to 511, as said below
- documents: int32 [131072], P(('dp', 'ctx')), may hold values from 0 to 131071, as said below
Outputs:
- attended: bfloat16 [131072, 1024], P(('dp', 'ctx'))
The draws below stay inside these ranges and needn't reach their ends.
Inputs may be any that keep to these rules, and one draw needn't show every extreme that they name: routing[r, 0] is the packed sequence and routing[r, 1] the position inside the 512-token block (the block at the owner's index along ctx) to which owner row r goes; every position is filled exactly once. Each aligned block of 32 rows of one owner goes, in order, to 32 consecutive positions of one destination, and different blocks of one owner go to different destinations. `documents`: A token's document id is 4096 times its packed sequence plus the position in that sequence at which its document begins; in every draw some sequence other than the last is one whole document, and every other sequence ends with a one-token document.
All inputs are finite; a program needn't handle non-finite values.
Results may differ from the reference program's by a relative error of at most 0.0045.
Values may be sent and summed in bfloat16 or wider, within the bound.
A program may use at most 64 MiB of HBM per device.

```python
import math
import jax
import jax.numpy as jnp
from jax import lax

H = 8
KVH = 1
HD = 128
TOK_DEV = 512
QPG = 8
CAP = 32
SEQ_LEN = 4096
TOKENS = 131072
N_DP = 32
N_CTX = 8


def layout(key):
    blocks = TOK_DEV // CAP
    column_keys = jax.random.split(jax.random.fold_in(key, 101), N_CTX)
    shifts = jax.vmap(lambda inner: jax.random.permutation(inner, N_DP))(column_keys).astype(jnp.int32)
    owner_rows = jnp.arange(TOKENS, dtype=jnp.int32)
    device = owner_rows // TOK_DEV
    owner = device // N_CTX
    column = device % N_CTX
    owner_slot = owner_rows % TOK_DEV
    owner_block = owner_slot // CAP
    within = owner_slot % CAP
    block_index = (owner_block - owner) % blocks
    target = (owner - shifts[column, block_index]) % N_DP
    position = block_index * CAP + within
    packed = target * SEQ_LEN + column * TOK_DEV + position
    return (target, position, packed)


def doc_layout(key):
    first_key, second_key, third_key = jax.random.split(jax.random.fold_in(key, 202), 3)
    reach = jax.random.randint(first_key, (N_DP, 1), 8, SEQ_LEN + 1)
    single = jax.random.randint(second_key, (), 0, N_DP - 1)
    spots = jnp.arange(SEQ_LEN, dtype=jnp.int32)
    sequence = jnp.arange(N_DP, dtype=jnp.int32)[:, None]
    begins = jax.random.randint(third_key, (N_DP, SEQ_LEN), 0, reach) == 0
    begins = begins | (spots[None, :] == SEQ_LEN - 1)
    begins = begins & (sequence != single)
    begins = begins | (spots[None, :] == 0)
    first = lax.cummax(jnp.where(begins, spots[None, :], 0), axis=1)
    return (sequence * SEQ_LEN + first).reshape(TOKENS)


def draw_routing(key, part):
    target, position, packed = layout(key)
    return jnp.stack([target, position], axis=1).astype(jnp.int32)


def draw_documents(key, part):
    target, position, packed = layout(key)
    doc_ids = doc_layout(key)
    return doc_ids[packed].astype(jnp.int32)


def draw_queries(key, part):
    target, position, packed = layout(key)
    key = jax.random.fold_in(key, 5)
    values = jax.random.truncated_normal(key, -6.0, 6.0, (TOKENS, KVH, QPG, HD), jnp.float32)
    return values.reshape(TOKENS, H * HD)[packed].astype(jnp.bfloat16)


def draw_keys_values(key, part):
    target, position, packed = layout(key)
    key = jax.random.fold_in(key, 7)
    key_part, value_part = jax.random.split(key)
    keys = jax.random.truncated_normal(key_part, -6.0, 6.0, (TOKENS, KVH, HD), jnp.float32)
    values = jax.random.truncated_normal(value_part, -6.0, 6.0, (TOKENS, KVH, HD), jnp.float32)
    stacked = jnp.stack([keys, values], axis=2)
    return stacked[packed].astype(jnp.bfloat16)


def setup_inputs(seed: int = 0) -> dict:
    splits = jax.random.split(jax.random.key(seed), 5)
    queries = draw_queries(jax.random.fold_in(splits[4], 71), 0)
    keys_values = draw_keys_values(jax.random.fold_in(splits[4], 71), 0)
    routing = draw_routing(jax.random.fold_in(splits[4], 71), 0)
    documents = draw_documents(jax.random.fold_in(splits[4], 71), 0)
    return dict(queries=queries, keys_values=keys_values, routing=routing, documents=documents)


def one_group(operands):
    group_q, group_k, group_v, doc_ids = operands
    factor = 1.0 / math.sqrt(HD)
    positions = jnp.arange(SEQ_LEN, dtype=jnp.int32)
    keys_f = group_k.astype(jnp.float32)
    values_f = group_v.astype(jnp.float32)

    def one_block(index):
        start = (index * TOK_DEV).astype(jnp.int32)
        block_q = lax.dynamic_slice_in_dim(group_q, start, TOK_DEV, 0)
        block_doc = lax.dynamic_slice_in_dim(doc_ids, start, TOK_DEV, 0)
        block_pos = start + jnp.arange(TOK_DEV, dtype=jnp.int32)
        scores = jnp.einsum('tqd,kd->qtk', block_q.astype(jnp.float32), keys_f) * factor
        allowed = (block_pos[:, None] >= positions[None, :]) & (block_doc[:, None] == doc_ids[None, :])
        scores = jnp.where(allowed[None], scores, -1e+30)
        peaks = lax.optimization_barrier(jnp.max(scores, axis=-1, keepdims=True))
        weights = jnp.where(allowed[None], jnp.exp(scores - peaks), 0.0)
        totals = lax.optimization_barrier(jnp.sum(weights, axis=-1))
        rounded = weights.astype(jnp.bfloat16)
        mixed = jnp.einsum('qtk,kd->tqd', rounded.astype(jnp.float32), values_f)
        return (mixed / jnp.transpose(totals)[:, :, None]).astype(jnp.bfloat16)
    blocks = lax.map(one_block, jnp.arange(N_CTX, dtype=jnp.int32))
    return blocks.reshape(SEQ_LEN, QPG, HD)

def reference(queries, keys_values, routing, documents):
    owner_rows = jnp.arange(TOKENS, dtype=jnp.int32)
    columns = owner_rows // TOK_DEV % N_CTX
    packed = (routing[:, 0] * SEQ_LEN + columns * TOK_DEV + routing[:, 1]).astype(jnp.int32)
    packed_q = jnp.zeros_like(queries).at[packed].set(queries)
    packed_kv = jnp.zeros_like(keys_values).at[packed].set(keys_values)
    packed_doc = jnp.zeros((TOKENS,), jnp.int32).at[packed].set(documents)
    group_q = packed_q.reshape(N_DP, SEQ_LEN, KVH, QPG, HD).transpose(0, 2, 1, 3, 4).reshape(N_DP * KVH, SEQ_LEN, QPG, HD)
    group_kv = packed_kv.reshape(N_DP, SEQ_LEN, KVH, 2, HD).transpose(0, 2, 1, 3, 4).reshape(N_DP * KVH, SEQ_LEN, 2, HD)
    group_doc = jnp.repeat(packed_doc.reshape(N_DP, SEQ_LEN), KVH, axis=0)
    results = lax.map(one_group, (group_q, group_kv[:, :, 0], group_kv[:, :, 1], group_doc))
    return results.reshape(N_DP, KVH, SEQ_LEN, QPG, HD).transpose(0, 2, 1, 3, 4).reshape(TOKENS, H * HD)
```

```python
import functools
import math

import jax
import jax.numpy as jnp
from jax import lax
from jax.experimental import pallas as pl
from jax.experimental.pallas import tpu as pltpu
from jax.sharding import PartitionSpec as P

MESH = pl.DeviceIdType.MESH
F32, BF16, I32 = jnp.float32, jnp.bfloat16, jnp.int32
DP, CTX = 32, 8
ROWS, HEADS, HD, CAP = 512, 8, 128, 32
BLOCKS = ROWS // CAP
PER = 2
CHUNKS = HEADS // PER
WIDE = PER * HD
TALL = PER * ROWS
SEQ = 4096
NEG = -1e30
FACTOR = math.log2(math.e) / math.sqrt(HD)


def kernel(
    key, labs, q_hbm, kv_hbm, out_hbm,
    q_v, kv_v, lab_s, lab_r, kv_s, kv_r, q_s, q_r,
    spread, gather, begin, k_all, v_all, q_two, scores, out_v,
    in_sem, lab_ss, lab_rs, kv_ss, kv_rs, q_ss, q_rs,
    k_ss, v_ss, k_rs, v_rs, out_sem,
):
    me, cx = lax.axis_index("dp"), lax.axis_index("ctx")
    y, low = cx // 2, cx % 2
    mate = y * 2 + (1 - low)

    barrier = pltpu.get_barrier_semaphore()

    def greet(j, _):
        pl.semaphore_signal(
            barrier, inc=1, device_id=((me + j) % DP, cx), device_id_type=MESH
        )
        return 0

    lax.fori_loop(1, DP, greet, 0)
    pl.semaphore_signal(barrier, inc=1, device_id=(me, mate), device_id_type=MESH)
    for dy in (1, 2, 3):
        pl.semaphore_signal(
            barrier, inc=1, device_id=(me, (y + dy) % 4 * 2 + low), device_id_type=MESH
        )

    get_kv = pltpu.make_async_copy(kv_hbm, kv_v, in_sem.at[0])
    get_q = pltpu.make_async_copy(q_hbm, q_v, in_sem.at[1])
    get_kv.start()
    get_q.start()
    lab_s[...] = labs[...]
    get_kv.wait()

    slots = DP * CAP
    spread[...] = jnp.where(
        key[...] == lax.broadcasted_iota(I32, (slots, ROWS), 0), 1.0, 0.0
    ).astype(BF16)

    def packed(x):
        part = jnp.dot(spread[...], x, preferred_element_type=F32)
        return part.astype(BF16).reshape(DP, CAP, x.shape[1])

    kv_s[...] = packed(kv_v[...])
    pl.semaphore_wait(barrier, DP - 1 + 4)

    def send_kv(j, _):
        there = ((me + j) % DP, cx)
        pltpu.make_async_remote_copy(
            lab_s.at[j], lab_r.at[j], lab_ss, lab_rs, device_id=there, device_id_type=MESH
        ).start()
        pltpu.make_async_remote_copy(
            kv_s.at[j], kv_r.at[j], kv_ss, kv_rs, device_id=there, device_id_type=MESH
        ).start()
        return 0

    lax.fori_loop(1, DP, send_kv, 0)
    lab_r[0] = lab_s[0]
    kv_r[0] = kv_s[0]
    get_q.wait()

    for ch in range(CHUNKS):

        q_s[ch] = packed(q_v[:, ch * WIDE : (ch + 1) * WIDE])

        def send_q(j, _):
            pltpu.make_async_remote_copy(
                q_s.at[ch, j], q_r.at[ch, j], q_ss.at[ch], q_rs.at[ch],
                device_id=((me + j) % DP, cx), device_id_type=MESH,
            ).start()
            return 0

        lax.fori_loop(1, DP, send_q, 0)
        q_r[ch, 0] = q_s[ch, 0]

    others = pl.ds(1, DP - 1)

    def group(src, dst, send, recv):
        return pltpu.make_async_remote_copy(
            src, dst, send, recv, device_id=((me + 1) % DP, cx), device_id_type=MESH
        )

    labels = group(lab_s.at[others], lab_r.at[others], lab_ss, lab_rs)
    labels.wait_recv()
    lab = lab_r[:, 0, :]
    lane = lax.broadcasted_iota(I32, (DP, HD), 1)
    place = jnp.sum(jnp.where(lane == CAP, lab, 0), axis=1, keepdims=True)
    slot = lax.broadcasted_iota(I32, (DP, HD), 0)
    place_row = jnp.sum(jnp.where(slot == lane, place, 0), axis=0, keepdims=True)
    block_row = lax.broadcasted_iota(I32, (ROWS, HD), 0) // CAP
    owner = jnp.where(place_row == block_row + 1, 1.0, 0.0).astype(BF16)
    widen = jnp.where(
        lax.broadcasted_iota(I32, (HD, slots), 1) // CAP
        == lax.broadcasted_iota(I32, (HD, slots), 0),
        1.0,
        0.0,
    ).astype(BF16)
    same = (
        lax.broadcasted_iota(I32, (ROWS, slots), 0) % CAP
        == lax.broadcasted_iota(I32, (ROWS, slots), 1) % CAP
    )
    gather[...] = jnp.where(
        same, jnp.dot(owner, widen, preferred_element_type=F32), 0.0
    ).astype(BF16)
    square = lax.broadcasted_iota(I32, (CAP, HD), 0) == lax.broadcasted_iota(I32, (CAP, HD), 1)
    for b in range(BLOCKS):
        row = jnp.sum(jnp.where(place == b + 1, lab, 0), axis=0, keepdims=True)
        column = jnp.sum(jnp.where(square, row, 0), axis=1, keepdims=True)
        begin[b * CAP : (b + 1) * CAP, :] = jnp.broadcast_to(column, (CAP, HD))

    def unpacked(x):
        return jnp.dot(gather[...], x.reshape(slots, x.shape[2]), preferred_element_type=F32)

    group(kv_s.at[others], kv_r.at[others], kv_ss, kv_rs).wait_recv()
    own = unpacked(kv_r[...])
    v_all[cx] = own[:, HD:].astype(BF16)
    k_all[cx] = jnp.transpose(own[:, :HD]).astype(BF16)

    def ctx_copies(n, block, there):
        return [
            pltpu.make_async_remote_copy(
                a.at[block], a.at[block], s.at[n], r.at[block],
                device_id=(me, there), device_id_type=MESH,
            )
            for a, s, r in ((k_all, k_ss, k_rs), (v_all, v_ss, v_rs))
        ]

    to_mate = (low == 0) | (y < 3)
    ups = [(dy, y + dy < 4, (y + dy) % 4 * 2 + low) for dy in (1, 2, 3)]

    @pl.when(to_mate)
    def _():
        for c in ctx_copies(0, cx, mate):
            c.start()

    for dy, live, there in ups:

        @pl.when(live)
        def _(dy=dy, there=there):
            for c in ctx_copies(dy, cx, there):
                c.start()

    @pl.when((low == 1) | (y < 3))
    def _():
        for c in ctx_copies(0, mate, mate):
            c.wait_recv()

    for dy, live, there in ups:

        @pl.when(live)
        def _(dy=dy, there=there):
            for c in ctx_copies(3 + dy, mate, there):
                c.start()

    ones = jnp.ones((ROWS, HD), BF16)
    key_lane = lax.broadcasted_iota(I32, (ROWS, ROWS), 1)
    key_sub = lax.broadcasted_iota(I32, (ROWS, ROWS), 0)

    def score(kb, diagonal):
        kt = k_all[kb]
        s = jnp.dot(
            q_two[...], jnp.concatenate([kt, kt], axis=0), preferred_element_type=F32
        )
        first = jnp.concatenate([begin[...]] * (ROWS // HD), axis=1)
        keep = key_lane + kb * ROWS >= first
        if diagonal:
            keep = keep & (key_lane <= key_sub)
        parts = [
            jnp.where(keep, s[h * ROWS : (h + 1) * ROWS], NEG) for h in range(PER)
        ]
        return jnp.concatenate(parts, axis=0)

    def widest(top, s):
        for i in range(ROWS // HD):
            top = jnp.maximum(top, s[:, i * HD : (i + 1) * HD])
        return top

    def chunk(ch, _):
        group(
            q_s.at[ch, others], q_r.at[ch, others], q_ss.at[ch], q_rs.at[ch]
        ).wait_recv()
        mine = unpacked(q_r[ch]) * FACTOR
        high = mine.astype(BF16)
        rest = (mine - high.astype(F32)).astype(BF16)
        for h in range(PER):
            at, cols = slice(h * ROWS, (h + 1) * ROWS), slice(h * HD, (h + 1) * HD)
            q_two[at, :HD] = high[:, cols]
            q_two[at, HD:] = rest[:, cols]
        s = score(cx, True)
        scores[0] = s
        top = widest(jnp.full((TALL, HD), NEG, F32), s)

        def first_pass(i, top):
            kb = cx - i

            @pl.when((ch == 0) & (kb // 2 < y))
            def _():
                for c in ctx_copies(0, kb, mate):
                    c.wait_recv()

            s = score(kb, False)
            scores[i] = s
            return widest(top, s)

        top = lax.fori_loop(1, cx + 1, first_pass, top)
        peak = jnp.max(top, axis=1, keepdims=True)

        def second_pass(i, total):
            w = jnp.exp2(scores[i] - peak).astype(BF16)
            v = jnp.concatenate([v_all[cx - i], ones], axis=1)
            return total + jnp.dot(w, v, preferred_element_type=F32)

        total = lax.fori_loop(0, cx + 1, second_pass, jnp.zeros((TALL, 2 * HD), F32))
        done = (total[:, :HD] / total[:, HD:]).astype(BF16)
        for h in range(PER):
            out_v[ch, :, h * HD : (h + 1) * HD] = done[h * ROWS : (h + 1) * ROWS]
        put(ch).start()
        return 0

    def put(ch):
        at = pl.ds(pl.multiple_of(ch * WIDE, WIDE), WIDE)
        return pltpu.make_async_copy(out_v.at[ch], out_hbm.at[:, at], out_sem.at[ch])

    lax.fori_loop(0, CHUNKS, chunk, 0)

    labels.wait_send()
    group(kv_s.at[others], kv_r.at[others], kv_ss, kv_rs).wait_send()
    for ch in range(CHUNKS):
        group(
            q_s.at[ch, others], q_r.at[ch, others], q_ss.at[ch], q_rs.at[ch]
        ).wait_send()

    @pl.when(to_mate)
    def _():
        for c in ctx_copies(0, cx, mate):
            c.wait_send()

    for dy, live, there in ups:

        @pl.when(live)
        def _(dy=dy, there=there):
            for c in ctx_copies(dy, cx, there):
                c.wait_send()
            for c in ctx_copies(3 + dy, mate, there):
                c.wait_send()

    for ch in range(CHUNKS):
        put(ch).wait()


def local(queries, keys_values, routing, documents):
    me = lax.axis_index("dp")
    head = routing.reshape(BLOCKS, CAP, 2)[:, 0, :]
    turn = (head[:, 0] - me) % DP
    hit = turn[None, :] == jnp.arange(DP, dtype=I32)[:, None]
    turns = (routing[:, 0] - me) % DP * CAP + jnp.arange(ROWS, dtype=I32) % CAP
    notes = jnp.concatenate(
        [documents.reshape(BLOCKS, CAP) % SEQ, head[:, 1:] // CAP + 1], axis=1
    )
    notes = jnp.pad(notes, ((0, 0), (0, HD - CAP - 1)))
    labs = jnp.sum(jnp.where(hit[:, :, None], notes[None], 0), axis=1)
    dma = pltpu.SemaphoreType.DMA
    vmem, anywhere = pl.BlockSpec(memory_space=pltpu.VMEM), pl.BlockSpec(memory_space=pl.ANY)
    return pl.pallas_call(
        kernel,
        out_shape=jax.ShapeDtypeStruct((ROWS, HEADS * HD), BF16),
        in_specs=[vmem, vmem, anywhere, anywhere],
        out_specs=anywhere,
        scratch_shapes=[
            pltpu.VMEM((ROWS, HEADS * HD), BF16),
            pltpu.VMEM((ROWS, 2 * HD), BF16),
            pltpu.VMEM((DP, 1, HD), I32),
            pltpu.VMEM((DP, 1, HD), I32),
            pltpu.VMEM((DP, CAP, 2 * HD), BF16),
            pltpu.VMEM((DP, CAP, 2 * HD), BF16),
            pltpu.VMEM((CHUNKS, DP, CAP, WIDE), BF16),
            pltpu.VMEM((CHUNKS, DP, CAP, WIDE), BF16),
            pltpu.VMEM((DP * CAP, ROWS), BF16),
            pltpu.VMEM((ROWS, DP * CAP), BF16),
            pltpu.VMEM((ROWS, HD), I32),
            pltpu.VMEM((CTX, HD, ROWS), BF16),
            pltpu.VMEM((CTX, ROWS, HD), BF16),
            pltpu.VMEM((TALL, 2 * HD), BF16),
            pltpu.VMEM((CTX, TALL, ROWS), F32),
            pltpu.VMEM((CHUNKS, ROWS, WIDE), BF16),
            dma((2,)), dma, dma, dma, dma, dma((CHUNKS,)), dma((CHUNKS,)),
            dma((7,)), dma((7,)), dma((CTX,)), dma((CTX,)), dma((CHUNKS,)),
        ],
        compiler_params=pltpu.CompilerParams(
            collective_id=1, has_side_effects=True, vmem_limit_bytes=56 << 20
        ),
        cost_estimate=pl.CostEstimate(
            flops=8 << 30, bytes_accessed=4 << 20, transcendentals=16 << 20
        ),
        name="relay_attend",
    )(turns.reshape(1, ROWS), labs.reshape(DP, 1, HD), queries, keys_values.reshape(ROWS, 2 * HD))


def solution(mesh):
    placed = (
        P(("dp", "ctx"), None),
        P(("dp", "ctx"), None, None, None),
        P(("dp", "ctx"), None),
        P(("dp", "ctx")),
    )
    return jax.shard_map(
        local, mesh=mesh, in_specs=placed, out_specs=P(("dp", "ctx"), None), check_vma=False
    )
```

```python
import functools
import math

import jax
import jax.numpy as jnp
from jax import lax
from jax.experimental import pallas as pl
from jax.experimental.pallas import tpu as pltpu
from jax.sharding import PartitionSpec as P

MESH = pl.DeviceIdType.MESH
F32, BF16, I32 = jnp.float32, jnp.bfloat16, jnp.int32
DP, CTX = 32, 8
ROWS, HEADS, HD, CAP = 512, 8, 128, 32
BLOCKS = ROWS // CAP
PER = 2
CHUNKS = HEADS // PER
WIDE = PER * HD
TALL = PER * ROWS
PAIR = 2 * ROWS
SEQ = 4096
NEG = -1e30
FACTOR = math.log2(math.e) / math.sqrt(HD)


def kernel(
    route_hbm, doc_hbm, q_hbm, kv_hbm, out_hbm,
    route_v, doc_v, q_v, kv_v, lab_s, lab_r, kv_s, kv_r, q_s, q_r,
    spread, gather, begin, k_all, v_all, q_two, scores, out_v,
    in_sem, lab_ss, lab_rs, kv_ss, kv_rs, q_ss, q_rs,
    k_ss, v_ss, k_rs, v_rs, out_sem,
):
    me, cx = lax.axis_index("dp"), lax.axis_index("ctx")
    y, low = cx // 2, cx % 2
    mate = y * 2 + (1 - low)

    barrier = pltpu.get_barrier_semaphore()

    def greet(j, _):
        pl.semaphore_signal(
            barrier, inc=1, device_id=((me + j) % DP, cx), device_id_type=MESH
        )
        return 0

    lax.fori_loop(1, DP, greet, 0)
    pl.semaphore_signal(barrier, inc=1, device_id=(me, mate), device_id_type=MESH)
    for dy in (1, 2, 3):
        pl.semaphore_signal(
            barrier, inc=1, device_id=(me, (y + dy) % 4 * 2 + low), device_id_type=MESH
        )

    gets = [
        pltpu.make_async_copy(a, b, in_sem.at[n])
        for n, (a, b) in enumerate(
            ((route_hbm, route_v), (doc_hbm, doc_v), (kv_hbm, kv_v), (q_hbm, q_v))
        )
    ]
    for get in gets:
        get.start()
    for get in gets[:2]:
        get.wait()
    turn = (route_v[0:1, :] - me) & (DP - 1)
    note = (doc_v[...] & (SEQ - 1)) * CAP + route_v[1:2, :] // CAP + 1
    key = turn * CAP + (lax.broadcasted_iota(I32, (1, ROWS), 1) & (CAP - 1))
    slots = DP * CAP
    spread[...] = jnp.where(
        key == lax.broadcasted_iota(I32, (slots, ROWS), 0), 1.0, 0.0
    ).astype(BF16)
    slot = lax.broadcasted_iota(I32, (DP, HD), 0)
    lane = lax.broadcasted_iota(I32, (DP, HD), 1)
    labs = jnp.zeros((DP, HD), I32)
    for i in range(ROWS // HD):
        part = slice(i * HD, (i + 1) * HD)
        labs = labs + jnp.where(turn[:, part] == slot, note[:, part], 0)
    for j in range(DP):
        lab_s[j] = labs[j : j + 1]
    gets[2].wait()

    def packed(x):
        part = jnp.dot(spread[...], x, preferred_element_type=F32)
        return part.astype(BF16).reshape(DP, CAP, x.shape[1])

    kv_s[...] = packed(jnp.concatenate([kv_v[:, 0, :], kv_v[:, 1, :]], axis=1))
    pl.semaphore_wait(barrier, DP - 1 + 4)

    def send_kv(j, _):
        there = ((me + j) % DP, cx)
        pltpu.make_async_remote_copy(
            lab_s.at[j], lab_r.at[j], lab_ss, lab_rs, device_id=there, device_id_type=MESH
        ).start()
        pltpu.make_async_remote_copy(
            kv_s.at[j], kv_r.at[j], kv_ss, kv_rs, device_id=there, device_id_type=MESH
        ).start()
        return 0

    lax.fori_loop(1, DP, send_kv, 0)
    lab_r[0] = lab_s[0]
    kv_r[0] = kv_s[0]
    gets[3].wait()

    def pack_q(ch):
        q_s[ch] = packed(q_v[:, ch * WIDE : (ch + 1) * WIDE])
        q_r[ch, 0] = q_s[ch, 0]

    def send_chunk(ch):
        def send_q(j, _):
            pltpu.make_async_remote_copy(
                q_s.at[ch, j], q_r.at[ch, j], q_ss.at[ch], q_rs.at[ch],
                device_id=((me + j) % DP, cx), device_id_type=MESH,
            ).start()
            return 0

        lax.fori_loop(1, DP, send_q, 0)

    pack_q(0)
    send_chunk(0)
    for ch in range(1, CHUNKS):
        pack_q(ch)
    others = pl.ds(1, DP - 1)

    def group(src, dst, send, recv):
        return pltpu.make_async_remote_copy(
            src, dst, send, recv, device_id=((me + 1) % DP, cx), device_id_type=MESH
        )

    labels = group(lab_s.at[others], lab_r.at[others], lab_ss, lab_rs)
    labels.wait_recv()
    lab = lab_r[:, 0, :]
    place = jnp.max(lab & (CAP - 1), axis=1, keepdims=True)
    place_row = jnp.sum(jnp.where(slot == lane, place, 0), axis=0, keepdims=True)
    block_row = lax.broadcasted_iota(I32, (ROWS, HD), 0) // CAP
    owner = jnp.where(place_row == block_row + 1, 1.0, 0.0).astype(BF16)
    widen = jnp.where(
        lax.broadcasted_iota(I32, (HD, slots), 1) // CAP
        == lax.broadcasted_iota(I32, (HD, slots), 0),
        1.0,
        0.0,
    ).astype(BF16)
    same = (
        lax.broadcasted_iota(I32, (ROWS, slots), 0) % CAP
        == lax.broadcasted_iota(I32, (ROWS, slots), 1) % CAP
    )
    gather[...] = jnp.where(
        same, jnp.dot(owner, widen, preferred_element_type=F32), 0.0
    ).astype(BF16)
    square = (lax.broadcasted_iota(I32, (CAP, HD), 1) & (CAP - 1)) == lax.broadcasted_iota(
        I32, (CAP, HD), 0
    )
    for b in range(BLOCKS):
        row = jnp.sum(jnp.where(place == b + 1, lab // CAP, 0), axis=0, keepdims=True)
        column = jnp.sum(jnp.where(square, row, 0), axis=1, keepdims=True)
        begin[b * CAP : (b + 1) * CAP, :] = jnp.broadcast_to(column, (CAP, HD))

    def unpacked(x):
        return jnp.dot(gather[...], x.reshape(slots, x.shape[2]), preferred_element_type=F32)

    group(kv_s.at[others], kv_r.at[others], kv_ss, kv_rs).wait_recv()
    own = unpacked(kv_r[...])
    v_all[cx] = own[:, HD:].astype(BF16)
    k_all[cx] = jnp.transpose(own[:, :HD]).astype(BF16)

    def ctx_copies(n, block, there):
        return [
            pltpu.make_async_remote_copy(
                a.at[block], a.at[block], s.at[n], r.at[block],
                device_id=(me, there), device_id_type=MESH,
            )
            for a, s, r in ((k_all, k_ss, k_rs), (v_all, v_ss, v_rs))
        ]

    ups = [(dy, y + dy < 4, (y + dy) % 4 * 2 + low) for dy in (1, 2, 3)]

    for c in ctx_copies(0, cx, mate):
        c.start()

    for dy, live, there in ups:

        @pl.when(live)
        def _(dy=dy, there=there):
            for c in ctx_copies(dy, cx, there):
                c.start()

    send_chunk(1)
    for c in ctx_copies(0, mate, mate):
        c.wait_recv()

    for dy, live, there in ups:

        @pl.when(live)
        def _(dy=dy, there=there):
            for c in ctx_copies(3 + dy, mate, there):
                c.start()

    send_chunk(2)
    send_chunk(3)
    ones = jnp.ones((PAIR, HD), BF16)
    key_lane = lax.broadcasted_iota(I32, (ROWS, PAIR), 1)
    query_row = lax.broadcasted_iota(I32, (ROWS, PAIR), 0) + low * ROWS

    def score(pair, diagonal):
        kt = jnp.concatenate([k_all[2 * pair], k_all[2 * pair + 1]], axis=1)
        s = jnp.dot(
            q_two[...], jnp.concatenate([kt, kt], axis=0), preferred_element_type=F32
        )
        first = jnp.concatenate([begin[...]] * (PAIR // HD), axis=1)
        keep = key_lane + pair * PAIR >= first
        if diagonal:
            keep = keep & (key_lane <= query_row)
        parts = [
            jnp.where(keep, s[h * ROWS : (h + 1) * ROWS], NEG) for h in range(PER)
        ]
        return jnp.concatenate(parts, axis=0)

    def widest(top, s):
        for i in range(PAIR // HD):
            top = jnp.maximum(top, s[:, i * HD : (i + 1) * HD])
        return top

    def chunk(ch, _):
        group(
            q_s.at[ch, others], q_r.at[ch, others], q_ss.at[ch], q_rs.at[ch]
        ).wait_recv()
        mine = unpacked(q_r[ch]) * FACTOR
        high = mine.astype(BF16)
        rest = (mine - high.astype(F32)).astype(BF16)
        for h in range(PER):
            at, cols = slice(h * ROWS, (h + 1) * ROWS), slice(h * HD, (h + 1) * HD)
            q_two[at, :HD] = high[:, cols]
            q_two[at, HD:] = rest[:, cols]
        s = score(y, True)
        scores[0] = s
        top = widest(jnp.full((TALL, HD), NEG, F32), s)

        def first_pass(i, top):
            pair = y - i

            @pl.when(ch == 0)
            def _():
                for block in (2 * pair, 2 * pair + 1):
                    for c in ctx_copies(0, block, mate):
                        c.wait_recv()

            s = score(pair, False)
            scores[i] = s
            return widest(top, s)

        top = lax.fori_loop(1, y + 1, first_pass, top)
        peak = jnp.max(top, axis=1, keepdims=True)

        def second_pass(i, total):
            w = jnp.exp2(scores[i] - peak).astype(BF16)
            pair = y - i
            v = jnp.concatenate([v_all[2 * pair], v_all[2 * pair + 1]], axis=0)
            v = jnp.concatenate([v, ones], axis=1)
            return total + jnp.dot(w, v, preferred_element_type=F32)

        total = lax.fori_loop(0, y + 1, second_pass, jnp.zeros((TALL, 2 * HD), F32))
        done = (total[:, :HD] / total[:, HD:]).astype(BF16)
        for h in range(PER):
            out_v[ch, :, h * HD : (h + 1) * HD] = done[h * ROWS : (h + 1) * ROWS]
        put(ch).start()
        return 0

    def put(ch):
        at = pl.ds(pl.multiple_of(ch * WIDE, WIDE), WIDE)
        return pltpu.make_async_copy(out_v.at[ch], out_hbm.at[:, at], out_sem.at[ch])

    lax.fori_loop(0, CHUNKS, chunk, 0)

    labels.wait_send()
    group(kv_s.at[others], kv_r.at[others], kv_ss, kv_rs).wait_send()
    for ch in range(CHUNKS):
        group(
            q_s.at[ch, others], q_r.at[ch, others], q_ss.at[ch], q_rs.at[ch]
        ).wait_send()

    for c in ctx_copies(0, cx, mate):
        c.wait_send()

    for dy, live, there in ups:

        @pl.when(live)
        def _(dy=dy, there=there):
            for c in ctx_copies(dy, cx, there):
                c.wait_send()
            for c in ctx_copies(3 + dy, mate, there):
                c.wait_send()

    for ch in range(CHUNKS):
        put(ch).wait()


def local(queries, keys_values, routing, documents):
    dma = pltpu.SemaphoreType.DMA
    anywhere = pl.BlockSpec(memory_space=pl.ANY)
    return pl.pallas_call(
        kernel,
        out_shape=jax.ShapeDtypeStruct((ROWS, HEADS * HD), BF16),
        in_specs=[anywhere] * 4,
        out_specs=anywhere,
        scratch_shapes=[
            pltpu.VMEM((2, ROWS), I32),
            pltpu.VMEM((1, ROWS), I32),
            pltpu.VMEM((ROWS, HEADS * HD), BF16),
            pltpu.VMEM((ROWS, 2, HD), BF16),
            pltpu.VMEM((DP, 1, HD), I32),
            pltpu.VMEM((DP, 1, HD), I32),
            pltpu.VMEM((DP, CAP, 2 * HD), BF16),
            pltpu.VMEM((DP, CAP, 2 * HD), BF16),
            pltpu.VMEM((CHUNKS, DP, CAP, WIDE), BF16),
            pltpu.VMEM((CHUNKS, DP, CAP, WIDE), BF16),
            pltpu.VMEM((DP * CAP, ROWS), BF16),
            pltpu.VMEM((ROWS, DP * CAP), BF16),
            pltpu.VMEM((ROWS, HD), I32),
            pltpu.VMEM((CTX, HD, ROWS), BF16),
            pltpu.VMEM((CTX, ROWS, HD), BF16),
            pltpu.VMEM((TALL, 2 * HD), BF16),
            pltpu.VMEM((CTX // 2, TALL, PAIR), F32),
            pltpu.VMEM((CHUNKS, ROWS, WIDE), BF16),
            dma((4,)), dma, dma, dma, dma, dma((CHUNKS,)), dma((CHUNKS,)),
            dma((7,)), dma((7,)), dma((CTX,)), dma((CTX,)), dma((CHUNKS,)),
        ],
        compiler_params=pltpu.CompilerParams(
            collective_id=1, has_side_effects=True, vmem_limit_bytes=56 << 20
        ),
        cost_estimate=pl.CostEstimate(
            flops=8 << 30, bytes_accessed=4 << 20, transcendentals=16 << 20
        ),
        name="relay_attend",
    )(routing.T, documents.reshape(1, ROWS), queries, keys_values.reshape(ROWS, 2, HD))


def solution(mesh):
    placed = (
        P(("dp", "ctx"), None),
        P(("dp", "ctx"), None, None, None),
        P(("dp", "ctx"), None),
        P(("dp", "ctx")),
    )
    return jax.shard_map(
        local, mesh=mesh, in_specs=placed, out_specs=P(("dp", "ctx"), None), check_vma=False
    )
```

```python
import functools
import math

import jax
import jax.numpy as jnp
from jax import lax
from jax.experimental import pallas as pl
from jax.experimental.pallas import tpu as pltpu
from jax.sharding import PartitionSpec as P

MESH = pl.DeviceIdType.MESH
F32, BF16, I32 = jnp.float32, jnp.bfloat16, jnp.int32
DP, CTX = 32, 8
ROWS, HEADS, HD, CAP = 512, 8, 128, 32
BLOCKS = ROWS // CAP
PER = 2
CHUNKS = HEADS // PER
WIDE = PER * HD
TALL = PER * ROWS
PAIR = 2 * ROWS
SEQ = 4096
NEG = -1e30
FACTOR = math.log2(math.e) / math.sqrt(HD)


def kernel(
    route_hbm, doc_hbm, q_hbm, kv_hbm, out,
    route_v, doc_v, q_v, kv_v, lab_s, lab_r, kv_s, kv_r, q_s, q_r,
    spread, gather, begin, k_all, v_all, q_two, bias, scores,
    in_sem, lab_ss, lab_rs, kv_ss, kv_rs, q_ss, q_rs,
    k_ss, v_ss, k_rs, v_rs,
):
    me, cx = lax.axis_index("dp"), lax.axis_index("ctx")
    y, low = cx // 2, cx % 2
    mate = y * 2 + (1 - low)

    barrier = pltpu.get_barrier_semaphore()

    def greet(j, _):
        pl.semaphore_signal(
            barrier, inc=1, device_id=((me + j) % DP, cx), device_id_type=MESH
        )
        return 0

    lax.fori_loop(1, DP, greet, 0)
    pl.semaphore_signal(barrier, inc=1, device_id=(me, mate), device_id_type=MESH)
    for dy in (1, 2, 3):
        pl.semaphore_signal(
            barrier, inc=1, device_id=(me, (y + dy) % 4 * 2 + low), device_id_type=MESH
        )

    gets = [
        pltpu.make_async_copy(a, b, in_sem.at[n])
        for n, (a, b) in enumerate(
            ((route_hbm, route_v), (doc_hbm, doc_v), (kv_hbm, kv_v), (q_hbm, q_v))
        )
    ]
    for get in gets:
        get.start()
    for get in gets[:2]:
        get.wait()
    turn = (route_v[0:1, :] - me) & (DP - 1)
    note = (doc_v[...] & (SEQ - 1)) * CAP + route_v[1:2, :] // CAP + 1
    key = turn * CAP + (lax.broadcasted_iota(I32, (1, ROWS), 1) & (CAP - 1))
    slots = DP * CAP
    spread[...] = jnp.where(
        key == lax.broadcasted_iota(I32, (slots, ROWS), 0), 1.0, 0.0
    ).astype(BF16)
    slot = lax.broadcasted_iota(I32, (DP, HD), 0)
    lane = lax.broadcasted_iota(I32, (DP, HD), 1)
    labs = jnp.zeros((DP, HD), I32)
    for i in range(ROWS // HD):
        part = slice(i * HD, (i + 1) * HD)
        labs = labs + jnp.where(turn[:, part] == slot, note[:, part], 0)
    for j in range(DP):
        lab_s[j] = labs[j : j + 1]
    gets[2].wait()

    def packed(x):
        part = jnp.dot(spread[...], x, preferred_element_type=F32)
        return part.astype(BF16).reshape(DP, CAP, x.shape[1])

    kv_s[...] = packed(jnp.concatenate([kv_v[:, 0, :], kv_v[:, 1, :]], axis=1))
    pl.semaphore_wait(barrier, DP - 1 + 4)

    def send_kv(j, _):
        there = ((me + j) % DP, cx)
        pltpu.make_async_remote_copy(
            lab_s.at[j], lab_r.at[j], lab_ss, lab_rs, device_id=there, device_id_type=MESH
        ).start()
        pltpu.make_async_remote_copy(
            kv_s.at[j], kv_r.at[j], kv_ss, kv_rs, device_id=there, device_id_type=MESH
        ).start()
        return 0

    lax.fori_loop(1, DP, send_kv, 0)
    lab_r[0] = lab_s[0]
    kv_r[0] = kv_s[0]
    gets[3].wait()

    def pack_q(ch):
        q_s[ch] = packed(q_v[:, ch * WIDE : (ch + 1) * WIDE])
        q_r[ch, 0] = q_s[ch, 0]

    def send_chunk(ch):
        def send_q(j, _):
            pltpu.make_async_remote_copy(
                q_s.at[ch, j], q_r.at[ch, j], q_ss.at[ch], q_rs.at[ch],
                device_id=((me + j) % DP, cx), device_id_type=MESH,
            ).start()
            return 0

        lax.fori_loop(1, DP, send_q, 0)

    others = pl.ds(1, DP - 1)

    def group(src, dst, send, recv):
        return pltpu.make_async_remote_copy(
            src, dst, send, recv, device_id=((me + 1) % DP, cx), device_id_type=MESH
        )

    def kv_group():
        return group(kv_s.at[others], kv_r.at[others], kv_ss, kv_rs)

    def q_group(ch):
        return group(q_s.at[ch, others], q_r.at[ch, others], q_ss.at[ch], q_rs.at[ch])

    for ch in range(CHUNKS):
        pack_q(ch)
    kv_group().wait_send()
    send_chunk(0)
    labels = group(lab_s.at[others], lab_r.at[others], lab_ss, lab_rs)
    labels.wait_recv()
    lab = lab_r[:, 0, :]
    place = jnp.max(lab & (CAP - 1), axis=1, keepdims=True)
    place_row = jnp.sum(jnp.where(slot == lane, place, 0), axis=0, keepdims=True)
    block_row = lax.broadcasted_iota(I32, (ROWS, HD), 0) // CAP
    owner = jnp.where(place_row == block_row + 1, 1.0, 0.0).astype(BF16)
    widen = jnp.where(
        lax.broadcasted_iota(I32, (HD, slots), 1) // CAP
        == lax.broadcasted_iota(I32, (HD, slots), 0),
        1.0,
        0.0,
    ).astype(BF16)
    same = (
        lax.broadcasted_iota(I32, (ROWS, slots), 0) % CAP
        == lax.broadcasted_iota(I32, (ROWS, slots), 1) % CAP
    )
    gather[...] = jnp.where(
        same, jnp.dot(owner, widen, preferred_element_type=F32), 0.0
    ).astype(BF16)
    square = (lax.broadcasted_iota(I32, (CAP, HD), 1) & (CAP - 1)) == lax.broadcasted_iota(
        I32, (CAP, HD), 0
    )
    for b in range(BLOCKS):
        row = jnp.sum(jnp.where(place == b + 1, lab // CAP, 0), axis=0, keepdims=True)
        column = jnp.sum(jnp.where(square, row, 0), axis=1, keepdims=True)
        begin[b * CAP : (b + 1) * CAP, :] = jnp.broadcast_to(column, (CAP, HD))

    def unpacked(x):
        return jnp.dot(gather[...], x.reshape(slots, x.shape[2]), preferred_element_type=F32)

    kv_group().wait_recv()
    own = unpacked(kv_r[...])
    v_all[cx] = own[:, HD:].astype(BF16)
    k_all[cx] = jnp.transpose(own[:, :HD]).astype(BF16)

    def ctx_copies(n, block, there):
        return [
            pltpu.make_async_remote_copy(
                a.at[block], a.at[block], s.at[n], r.at[block],
                device_id=(me, there), device_id_type=MESH,
            )
            for a, s, r in ((k_all, k_ss, k_rs), (v_all, v_ss, v_rs))
        ]

    ups = [(n, n > y, n * 2 + low) for n in (3, 2, 1)]

    for c in ctx_copies(0, cx, mate):
        c.start()

    for n, live, there in ups:

        @pl.when(live)
        def _(n=n, there=there):
            for c in ctx_copies(n, cx, there):
                c.start()

    for c in ctx_copies(0, mate, mate):
        c.wait_recv()

    for n, live, there in ups:

        @pl.when(live)
        def _(n=n, there=there):
            for c in ctx_copies(3 + n, mate, there):
                c.start()

    send_chunk(1)
    key_lane = lax.broadcasted_iota(I32, (ROWS, PAIR), 1)
    query_row = lax.broadcasted_iota(I32, (ROWS, PAIR), 0) + cx * ROWS
    first = jnp.concatenate([begin[...]] * (PAIR // HD), axis=1)

    def draw_mask(i, _):
        key_pos = key_lane + (y - i) * PAIR
        keep = (key_pos >= first) & (key_pos <= query_row)
        bias[i] = jnp.where(keep, 0.0, NEG)
        return 0

    lax.fori_loop(0, y + 1, draw_mask, 0)
    q_group(0).wait_send()
    send_chunk(2)
    q_group(1).wait_send()
    send_chunk(3)
    ones = jnp.ones((PAIR, HD), BF16)
    def score(i):
        pair = y - i
        kt = jnp.concatenate([k_all[2 * pair], k_all[2 * pair + 1]], axis=1)
        s = jnp.dot(
            q_two[...], jnp.concatenate([kt, kt], axis=0), preferred_element_type=F32
        )
        return s + jnp.concatenate([bias[i]] * PER, axis=0)

    def widest(top, s):
        for i in range(PAIR // HD):
            top = jnp.maximum(top, s[:, i * HD : (i + 1) * HD])
        return top

    def chunk(ch, _):
        q_group(ch).wait_recv()
        mine = unpacked(q_r[ch]) * FACTOR
        high = mine.astype(BF16)
        rest = (mine - high.astype(F32)).astype(BF16)
        for h in range(PER):
            at, cols = slice(h * ROWS, (h + 1) * ROWS), slice(h * HD, (h + 1) * HD)
            q_two[at, :HD] = high[:, cols]
            q_two[at, HD:] = rest[:, cols]
        def first_pass(i, top):
            pair = y - i

            @pl.when((ch == 0) & (i > 0))
            def _():
                for block in (2 * pair, 2 * pair + 1):
                    for c in ctx_copies(0, block, mate):
                        c.wait_recv()

            s = score(i)
            scores[i] = s
            return widest(top, s)

        top = lax.fori_loop(
            0, y + 1, first_pass, jnp.full((TALL, HD), NEG, F32)
        )
        peak = jnp.max(top, axis=1, keepdims=True)

        def second_pass(i, total):
            w = jnp.exp2(scores[i] - peak).astype(BF16)
            pair = y - i
            v = jnp.concatenate([v_all[2 * pair], v_all[2 * pair + 1]], axis=0)
            v = jnp.concatenate([v, ones], axis=1)
            return total + jnp.dot(w, v, preferred_element_type=F32)

        total = lax.fori_loop(0, y + 1, second_pass, jnp.zeros((TALL, 2 * HD), F32))
        done = (total[:, :HD] / total[:, HD:]).astype(BF16)
        for h in range(PER):
            at = pl.ds(pl.multiple_of(ch * WIDE + h * HD, HD), HD)
            out[:, at] = done[h * ROWS : (h + 1) * ROWS]
        return 0

    lax.fori_loop(0, CHUNKS, chunk, 0)

    labels.wait_send()
    q_group(2).wait_send()
    q_group(3).wait_send()

    for c in ctx_copies(0, cx, mate):
        c.wait_send()

    for n, live, there in ups:

        @pl.when(live)
        def _(n=n, there=there):
            for c in ctx_copies(n, cx, there):
                c.wait_send()
            for c in ctx_copies(3 + n, mate, there):
                c.wait_send()


def local(queries, keys_values, routing, documents):
    dma = pltpu.SemaphoreType.DMA
    anywhere = pl.BlockSpec(memory_space=pl.ANY)
    return pl.pallas_call(
        kernel,
        out_shape=pltpu.VMEM((ROWS, HEADS * HD), BF16),
        in_specs=[anywhere] * 4,
        out_specs=pl.BlockSpec(memory_space=pltpu.VMEM),
        scratch_shapes=[
            pltpu.VMEM((2, ROWS), I32),
            pltpu.VMEM((1, ROWS), I32),
            pltpu.VMEM((ROWS, HEADS * HD), BF16),
            pltpu.VMEM((ROWS, 2, HD), BF16),
            pltpu.VMEM((DP, 1, HD), I32),
            pltpu.VMEM((DP, 1, HD), I32),
            pltpu.VMEM((DP, CAP, 2 * HD), BF16),
            pltpu.VMEM((DP, CAP, 2 * HD), BF16),
            pltpu.VMEM((CHUNKS, DP, CAP, WIDE), BF16),
            pltpu.VMEM((CHUNKS, DP, CAP, WIDE), BF16),
            pltpu.VMEM((DP * CAP, ROWS), BF16),
            pltpu.VMEM((ROWS, DP * CAP), BF16),
            pltpu.VMEM((ROWS, HD), I32),
            pltpu.VMEM((CTX, HD, ROWS), BF16),
            pltpu.VMEM((CTX, ROWS, HD), BF16),
            pltpu.VMEM((TALL, 2 * HD), BF16),
            pltpu.VMEM((CTX // 2, ROWS, PAIR), F32),
            pltpu.VMEM((CTX // 2, TALL, PAIR), F32),
            dma((4,)), dma, dma, dma, dma, dma((CHUNKS,)), dma((CHUNKS,)),
            dma((7,)), dma((7,)), dma((CTX,)), dma((CTX,)),
        ],
        compiler_params=pltpu.CompilerParams(
            collective_id=1, has_side_effects=True, vmem_limit_bytes=56 << 20
        ),
        cost_estimate=pl.CostEstimate(
            flops=8 << 30, bytes_accessed=4 << 20, transcendentals=16 << 20
        ),
        name="relay_attend",
    )(routing.T, documents.reshape(1, ROWS), queries, keys_values.reshape(ROWS, 2, HD))


def solution(mesh):
    placed = (
        P(("dp", "ctx"), None),
        P(("dp", "ctx"), None, None, None),
        P(("dp", "ctx"), None),
        P(("dp", "ctx")),
    )
    return jax.shard_map(
        local, mesh=mesh, in_specs=placed, out_specs=P(("dp", "ctx"), None), check_vma=False
    )
```

```python
import functools
import math

import jax
import jax.numpy as jnp
from jax import lax
from jax.experimental import pallas as pl
from jax.experimental.pallas import tpu as pltpu
from jax.sharding import PartitionSpec as P

MESH = pl.DeviceIdType.MESH
F32, BF16, I32 = jnp.float32, jnp.bfloat16, jnp.int32
DP, CTX = 32, 8
ROWS, HEADS, HD, CAP = 512, 8, 128, 32
BLOCKS = ROWS // CAP
SIZES = (2, 2, 2, 1, 1)
STARTS = (0, 2, 4, 6, 7)
MOST = 2
CHUNKS = len(SIZES)
SUMS = HD + 16
PAIR = 2 * ROWS
SEQ = 4096
NEG = -1e30
FACTOR = math.log2(math.e) / math.sqrt(HD)


def kernel(
    route_hbm, doc_hbm, q_hbm, kv_hbm, out,
    route_v, doc_v, q_v, kv_v, lab_s, lab_r, kv_s, kv_r, q_s2, q_r2, q_s1, q_r1,
    spread, gather, begin, k_all, v_all, q_cols, bias, scores,
    in_sem, lab_ss, lab_rs, kv_ss, kv_rs, q_ss, q_rs,
    k_ss, v_ss, k_rs, v_rs,
):
    me, cx = lax.axis_index("dp"), lax.axis_index("ctx")
    y, low = cx // 2, cx % 2
    mate = y * 2 + (1 - low)

    barrier = pltpu.get_barrier_semaphore()

    def greet(j, _):
        pl.semaphore_signal(
            barrier, inc=1, device_id=((me + j) & (DP - 1), cx), device_id_type=MESH
        )
        return 0

    lax.fori_loop(1, DP, greet, 0)
    pl.semaphore_signal(barrier, inc=1, device_id=(me, mate), device_id_type=MESH)
    for dy in (1, 2, 3):
        pl.semaphore_signal(
            barrier, inc=1, device_id=(me, (y + dy) % 4 * 2 + low), device_id_type=MESH
        )

    gets = [
        pltpu.make_async_copy(a, b, in_sem.at[n])
        for n, (a, b) in enumerate(
            ((route_hbm, route_v), (doc_hbm, doc_v), (kv_hbm, kv_v), (q_hbm, q_v))
        )
    ]
    for get in gets:
        get.start()
    for get in gets[:2]:
        get.wait()
    turn = (route_v[0:1, :] - me) & (DP - 1)
    note = (doc_v[...] & (SEQ - 1)) * CAP + route_v[1:2, :] // CAP + 1
    key = turn * CAP + (lax.broadcasted_iota(I32, (1, ROWS), 1) & (CAP - 1))
    slots = DP * CAP
    spread[...] = jnp.where(
        key == lax.broadcasted_iota(I32, (slots, ROWS), 0), 1.0, 0.0
    ).astype(BF16)
    slot = lax.broadcasted_iota(I32, (DP, HD), 0)
    lane = lax.broadcasted_iota(I32, (DP, HD), 1)
    labs = jnp.zeros((DP, HD), I32)
    for i in range(ROWS // HD):
        part = slice(i * HD, (i + 1) * HD)
        labs = labs + jnp.where(turn[:, part] == slot, note[:, part], 0)
    for j in range(DP):
        lab_s[j] = labs[j : j + 1]
    gets[2].wait()

    def packed(x):
        part = jnp.dot(spread[...], x, preferred_element_type=F32)
        return part.astype(BF16).reshape(DP, CAP, x.shape[1])

    kv_s[...] = packed(jnp.concatenate([kv_v[:, 0, :], kv_v[:, 1, :]], axis=1))
    pl.semaphore_wait(barrier, DP - 1 + 4)

    def send_kv(j, _):
        there = ((me + j) & (DP - 1), cx)
        pltpu.make_async_remote_copy(
            lab_s.at[j], lab_r.at[j], lab_ss, lab_rs, device_id=there, device_id_type=MESH
        ).start()
        pltpu.make_async_remote_copy(
            kv_s.at[j], kv_r.at[j], kv_ss, kv_rs, device_id=there, device_id_type=MESH
        ).start()
        return 0

    lax.fori_loop(1, DP, send_kv, 0)
    lab_r[0] = lab_s[0]
    kv_r[0] = kv_s[0]
    gets[3].wait()

    def q_bufs(ch):
        if SIZES[ch] == 2:
            return q_s2.at[ch], q_r2.at[ch]
        return q_s1.at[ch - 3], q_r1.at[ch - 3]

    def pack_q(ch):
        held, got = q_bufs(ch)
        held[...] = packed(q_v[:, STARTS[ch] * HD : (STARTS[ch] + SIZES[ch]) * HD])
        got[0] = held[0]

    def send_chunk(ch):
        held, got = q_bufs(ch)

        def send_q(j, _):
            pltpu.make_async_remote_copy(
                held.at[j], got.at[j], q_ss.at[ch], q_rs.at[ch],
                device_id=((me + j) & (DP - 1), cx), device_id_type=MESH,
            ).start()
            return 0

        lax.fori_loop(1, DP, send_q, 0)

    others = pl.ds(1, DP - 1)

    def group(src, dst, send, recv):
        return pltpu.make_async_remote_copy(
            src, dst, send, recv, device_id=((me + 1) % DP, cx), device_id_type=MESH
        )

    def kv_group():
        return group(kv_s.at[others], kv_r.at[others], kv_ss, kv_rs)

    def q_group(ch):
        held, got = q_bufs(ch)
        return group(held.at[others], got.at[others], q_ss.at[ch], q_rs.at[ch])

    for ch in range(CHUNKS):
        pack_q(ch)
    send_chunk(0)
    kv_group().wait_send()
    labels = group(lab_s.at[others], lab_r.at[others], lab_ss, lab_rs)
    labels.wait_recv()
    lab = lab_r[:, 0, :]
    place = jnp.max(lab & (CAP - 1), axis=1, keepdims=True)
    place_row = jnp.sum(jnp.where(slot == lane, place, 0), axis=0, keepdims=True)
    block_row = lax.broadcasted_iota(I32, (ROWS, HD), 0) // CAP
    owner = jnp.where(place_row == block_row + 1, 1.0, 0.0).astype(BF16)
    widen = jnp.where(
        lax.broadcasted_iota(I32, (HD, slots), 1) // CAP
        == lax.broadcasted_iota(I32, (HD, slots), 0),
        1.0,
        0.0,
    ).astype(BF16)
    same = (
        lax.broadcasted_iota(I32, (ROWS, slots), 0) % CAP
        == lax.broadcasted_iota(I32, (ROWS, slots), 1) % CAP
    )
    gather[...] = jnp.where(
        same, jnp.dot(owner, widen, preferred_element_type=F32), 0.0
    ).astype(BF16)
    square = (lax.broadcasted_iota(I32, (CAP, HD), 1) & (CAP - 1)) == lax.broadcasted_iota(
        I32, (CAP, HD), 0
    )
    for b in range(BLOCKS):
        row = jnp.sum(jnp.where(place == b + 1, lab // CAP, 0), axis=0, keepdims=True)
        column = jnp.sum(jnp.where(square, row, 0), axis=1, keepdims=True)
        begin[b * CAP : (b + 1) * CAP, :] = jnp.broadcast_to(column.astype(F32), (CAP, HD))

    def unpacked(x):
        return jnp.dot(gather[...], x.reshape(slots, x.shape[2]), preferred_element_type=F32)

    kv_group().wait_recv()
    own = unpacked(kv_r[...])
    k_all[cx] = own[:, :HD].astype(BF16)
    v_all[cx] = jnp.transpose(own[:, HD:]).astype(BF16)

    def ctx_copies(n, block, there):
        return [
            pltpu.make_async_remote_copy(
                a.at[block], a.at[block], s.at[n], r.at[block],
                device_id=(me, there), device_id_type=MESH,
            )
            for a, s, r in ((k_all, k_ss, k_rs), (v_all, v_ss, v_rs))
        ]

    ups = [(n, n > y, n * 2 + low) for n in (3, 2, 1)]

    for a, s, r in ((k_all, k_ss, k_rs), (v_all, v_ss, v_rs)):
        step_rows = a.shape[1] // 4
        for i in range(4):
            piece = a.at[cx, pl.ds(i * step_rows, step_rows)]
            pltpu.make_async_remote_copy(
                piece, piece, s.at[0], r.at[cx], device_id=(me, mate), device_id_type=MESH
            ).start()

    def send_up(base, block):
        for part in (0, 1):
            for n, live, there in ups:

                @pl.when(live)
                def _(n=n, there=there, part=part):
                    ctx_copies(base + n, block, there)[part].start()

    send_up(0, cx)
    for c in ctx_copies(0, mate, mate):
        c.wait_recv()

    send_up(3, mate)
    for c in ctx_copies(0, cx, mate):
        c.wait_send()
    send_chunk(1)
    first = jnp.transpose(begin[...])[0:1, :].astype(I32)
    last = lax.broadcasted_iota(I32, (1, ROWS), 1) + cx * ROWS
    key_row = lax.broadcasted_iota(I32, (PAIR, ROWS), 0)

    def draw_mask(i, _):
        start = (y - i) * PAIR
        keep = (key_row >= first - start) & (key_row <= last - start)
        bias[i] = jnp.where(keep, 0.0, NEG)
        return 0

    lax.fori_loop(0, y + 1, draw_mask, 0)
    q_group(0).wait_send()
    send_chunk(2)
    ones = jnp.ones((SUMS - HD, PAIR), BF16)

    def attend(got, start, size, await_keys):
        width = size * ROWS
        mine = unpacked(got) * FACTOR
        for h in range(size):
            x = jnp.transpose(mine[:, h * HD : (h + 1) * HD])
            high = x.astype(BF16)
            at = slice(h * ROWS, (h + 1) * ROWS)
            q_cols[:HD, at] = high
            q_cols[HD:, at] = (x - high.astype(F32)).astype(BF16)

        def await_pair(i, part):
            @pl.when(await_keys & (i > 0))
            def _():
                for block in (2 * (y - i), 2 * (y - i) + 1):
                    ctx_copies(0, block, mate)[part].wait_recv()

        def first_pass(i, top):
            pair = y - i

            await_pair(i, 0)
            k = jnp.concatenate([k_all[2 * pair], k_all[2 * pair + 1]], axis=0)
            s = jnp.dot(
                jnp.concatenate([k, k], axis=1), q_cols[:, :width],
                preferred_element_type=F32,
            ) + jnp.concatenate([bias[i]] * size, axis=1)
            scores[i, :, :width] = s
            return jnp.maximum(top, jnp.max(s.reshape(PAIR // 8, 8, width), axis=0))

        top = lax.fori_loop(0, y + 1, first_pass, jnp.full((8, width), NEG, F32))
        peak = jnp.max(top, axis=0, keepdims=True)

        def second_pass(i, total):
            pair = y - i
            await_pair(i, 1)
            w = jnp.exp2(scores[i, :, :width] - peak).astype(BF16)
            v = jnp.concatenate([v_all[2 * pair], v_all[2 * pair + 1]], axis=1)
            v = jnp.concatenate([v, ones], axis=0)
            return total + jnp.dot(v, w, preferred_element_type=F32)

        total = lax.fori_loop(0, y + 1, second_pass, jnp.zeros((SUMS, width), F32))
        done = total[:HD] / total[HD : HD + 1]
        for h in range(size):
            at = pl.ds(pl.multiple_of((start + h) * HD, HD), HD)
            out[:, at] = jnp.transpose(done[:, h * ROWS : (h + 1) * ROWS]).astype(BF16)

    def double(ch, _):
        held, got = q_s2.at[ch], q_r2.at[ch]
        group(held.at[others], got.at[others], q_ss.at[ch], q_rs.at[ch]).wait_recv()

        @pl.when(ch == 1)
        def _():
            send_chunk(3)

        @pl.when(ch == 2)
        def _():
            send_chunk(4)

        attend(q_r2[ch], 2 * ch, 2, ch == 0)
        return 0

    def single(n, _):
        held, got = q_s1.at[n], q_r1.at[n]
        group(held.at[others], got.at[others], q_ss.at[n + 3], q_rs.at[n + 3]).wait_recv()
        attend(q_r1[n], n + 6, 1, n < 0)
        return 0

    lax.fori_loop(0, 3, double, 0)
    lax.fori_loop(0, 2, single, 0)

    labels.wait_send()
    for ch in range(1, CHUNKS):
        q_group(ch).wait_send()


    for n, live, there in ups:

        @pl.when(live)
        def _(n=n, there=there):
            for c in ctx_copies(n, cx, there):
                c.wait_send()
            for c in ctx_copies(3 + n, mate, there):
                c.wait_send()


def local(queries, keys_values, routing, documents):
    dma = pltpu.SemaphoreType.DMA
    anywhere = pl.BlockSpec(memory_space=pl.ANY)
    return pl.pallas_call(
        kernel,
        out_shape=pltpu.VMEM((ROWS, HEADS * HD), BF16),
        in_specs=[anywhere] * 4,
        out_specs=pl.BlockSpec(memory_space=pltpu.VMEM),
        scratch_shapes=[
            pltpu.VMEM((2, ROWS), I32),
            pltpu.VMEM((1, ROWS), I32),
            pltpu.VMEM((ROWS, HEADS * HD), BF16),
            pltpu.VMEM((ROWS, 2, HD), BF16),
            pltpu.VMEM((DP, 1, HD), I32),
            pltpu.VMEM((DP, 1, HD), I32),
            pltpu.VMEM((DP, CAP, 2 * HD), BF16),
            pltpu.VMEM((DP, CAP, 2 * HD), BF16),
            pltpu.VMEM((3, DP, CAP, 2 * HD), BF16),
            pltpu.VMEM((3, DP, CAP, 2 * HD), BF16),
            pltpu.VMEM((2, DP, CAP, HD), BF16),
            pltpu.VMEM((2, DP, CAP, HD), BF16),
            pltpu.VMEM((DP * CAP, ROWS), BF16),
            pltpu.VMEM((ROWS, DP * CAP), BF16),
            pltpu.VMEM((ROWS, HD), F32),
            pltpu.VMEM((CTX, ROWS, HD), BF16),
            pltpu.VMEM((CTX, HD, ROWS), BF16),
            pltpu.VMEM((2 * HD, MOST * ROWS), BF16),
            pltpu.VMEM((CTX // 2, PAIR, ROWS), F32),
            pltpu.VMEM((CTX // 2, PAIR, MOST * ROWS), F32),
            dma((4,)), dma, dma, dma, dma, dma((CHUNKS,)), dma((CHUNKS,)),
            dma((7,)), dma((7,)), dma((CTX,)), dma((CTX,)),
        ],
        compiler_params=pltpu.CompilerParams(
            collective_id=1, has_side_effects=True, vmem_limit_bytes=56 << 20
        ),
        cost_estimate=pl.CostEstimate(
            flops=8 << 30, bytes_accessed=4 << 20, transcendentals=16 << 20
        ),
        name="relay_attend",
    )(routing.T, documents.reshape(1, ROWS), queries, keys_values.reshape(ROWS, 2, HD))


def solution(mesh):
    placed = (
        P(("dp", "ctx"), None),
        P(("dp", "ctx"), None, None, None),
        P(("dp", "ctx"), None),
        P(("dp", "ctx")),
    )
    return jax.shard_map(
        local, mesh=mesh, in_specs=placed, out_specs=P(("dp", "ctx"), None), check_vma=False
    )
```

```python
import functools
import math

import jax
import jax.numpy as jnp
from jax import lax
from jax.experimental import pallas as pl
from jax.experimental.pallas import tpu as pltpu
from jax.sharding import PartitionSpec as P

MESH = pl.DeviceIdType.MESH
F32, BF16, I32 = jnp.float32, jnp.bfloat16, jnp.int32
DP, CTX = 32, 8
ROWS, HEADS, HD, CAP = 512, 8, 128, 32
BLOCKS = ROWS // CAP
SIZES = (2, 2, 2, 1, 1)
STARTS = (0, 2, 4, 6, 7)
MOST = 2
CHUNKS = len(SIZES)
SUMS = HD + 16
PAIR = 2 * ROWS
SEQ = 4096
NEG = -1e30
FACTOR = math.log2(math.e) / math.sqrt(HD)


def kernel(
    route_hbm, doc_hbm, q_hbm, kv_hbm, out,
    route_v, doc_v, q_v, kv_v, lab_s, lab_r, kv_s, kv_r, q_s2, q_r2, q_s1, q_r1,
    spread, gather, begin, k_all, v_all, q_cols, bias, scores,
    in_sem, lab_ss, lab_rs, kv_ss, kv_rs, q_ss, q_rs,
    k_ss, v_ss, k_rs, v_rs,
):
    me, cx = lax.axis_index("dp"), lax.axis_index("ctx")
    y, low = cx // 2, cx % 2
    mate = y * 2 + (1 - low)

    barrier = pltpu.get_barrier_semaphore()

    def greet(j, _):
        pl.semaphore_signal(
            barrier, inc=1, device_id=((me + j) & (DP - 1), cx), device_id_type=MESH
        )
        return 0

    lax.fori_loop(1, DP, greet, 0)
    pl.semaphore_signal(barrier, inc=1, device_id=(me, mate), device_id_type=MESH)
    for dy in (1, 2, 3):
        pl.semaphore_signal(
            barrier, inc=1, device_id=(me, (y + dy) % 4 * 2 + low), device_id_type=MESH
        )

    gets = [
        pltpu.make_async_copy(a, b, in_sem.at[n])
        for n, (a, b) in enumerate(
            ((route_hbm, route_v), (doc_hbm, doc_v), (kv_hbm, kv_v), (q_hbm, q_v))
        )
    ]
    for get in gets:
        get.start()
    for get in gets[:2]:
        get.wait()
    turn = (route_v[0:1, :] - me) & (DP - 1)
    note = (doc_v[...] & (SEQ - 1)) * CAP + route_v[1:2, :] // CAP + 1
    key = turn * CAP + (lax.broadcasted_iota(I32, (1, ROWS), 1) & (CAP - 1))
    slots = DP * CAP
    spread[...] = jnp.where(
        key == lax.broadcasted_iota(I32, (slots, ROWS), 0), 1.0, 0.0
    ).astype(BF16)
    slot = lax.broadcasted_iota(I32, (DP, HD), 0)
    lane = lax.broadcasted_iota(I32, (DP, HD), 1)
    labs = jnp.zeros((DP, HD), I32)
    for i in range(ROWS // HD):
        part = slice(i * HD, (i + 1) * HD)
        labs = labs + jnp.where(turn[:, part] == slot, note[:, part], 0)
    for j in range(DP):
        lab_s[j] = labs[j : j + 1]
    gets[2].wait()

    def packed(x):
        part = jnp.dot(spread[...], x, preferred_element_type=F32)
        return part.astype(BF16).reshape(DP, CAP, x.shape[1])

    kv_s[...] = packed(jnp.concatenate([kv_v[:, 0, :], kv_v[:, 1, :]], axis=1))
    pl.semaphore_wait(barrier, DP - 1 + 4)

    def send_kv(j, _):
        there = ((me + j) & (DP - 1), cx)
        pltpu.make_async_remote_copy(
            lab_s.at[j], lab_r.at[j], lab_ss, lab_rs, device_id=there, device_id_type=MESH
        ).start()
        pltpu.make_async_remote_copy(
            kv_s.at[j], kv_r.at[j], kv_ss, kv_rs, device_id=there, device_id_type=MESH
        ).start()
        return 0

    lax.fori_loop(1, DP, send_kv, 0)
    lab_r[0] = lab_s[0]
    kv_r[0] = kv_s[0]
    gets[3].wait()

    def q_bufs(ch):
        if SIZES[ch] == 2:
            return q_s2.at[ch], q_r2.at[ch]
        return q_s1.at[ch - 3], q_r1.at[ch - 3]

    def pack_q(ch):
        held, got = q_bufs(ch)
        held[...] = packed(q_v[:, STARTS[ch] * HD : (STARTS[ch] + SIZES[ch]) * HD])
        got[0] = held[0]

    def send_chunk(ch):
        held, got = q_bufs(ch)

        def send_q(j, _):
            pltpu.make_async_remote_copy(
                held.at[j], got.at[j], q_ss.at[ch], q_rs.at[ch],
                device_id=((me + j) & (DP - 1), cx), device_id_type=MESH,
            ).start()
            return 0

        lax.fori_loop(1, DP, send_q, 0)

    others = pl.ds(1, DP - 1)

    def group(src, dst, send, recv):
        return pltpu.make_async_remote_copy(
            src, dst, send, recv, device_id=((me + 1) % DP, cx), device_id_type=MESH
        )

    def kv_group():
        return group(kv_s.at[others], kv_r.at[others], kv_ss, kv_rs)

    def q_group(ch):
        held, got = q_bufs(ch)
        return group(held.at[others], got.at[others], q_ss.at[ch], q_rs.at[ch])

    for ch in range(CHUNKS):
        pack_q(ch)
    send_chunk(0)
    kv_group().wait_send()
    labels = group(lab_s.at[others], lab_r.at[others], lab_ss, lab_rs)
    labels.wait_recv()
    lab = lab_r[:, 0, :]
    place = jnp.max(lab & (CAP - 1), axis=1, keepdims=True)
    place_row = jnp.sum(jnp.where(slot == lane, place, 0), axis=0, keepdims=True)
    block_row = lax.broadcasted_iota(I32, (ROWS, HD), 0) // CAP
    owner = jnp.where(place_row == block_row + 1, 1.0, 0.0).astype(BF16)
    widen = jnp.where(
        lax.broadcasted_iota(I32, (HD, slots), 1) // CAP
        == lax.broadcasted_iota(I32, (HD, slots), 0),
        1.0,
        0.0,
    ).astype(BF16)
    same = (
        lax.broadcasted_iota(I32, (ROWS, slots), 0) % CAP
        == lax.broadcasted_iota(I32, (ROWS, slots), 1) % CAP
    )
    gather[...] = jnp.where(
        same, jnp.dot(owner, widen, preferred_element_type=F32), 0.0
    ).astype(BF16)
    square = (lax.broadcasted_iota(I32, (CAP, HD), 1) & (CAP - 1)) == lax.broadcasted_iota(
        I32, (CAP, HD), 0
    )
    for b in range(BLOCKS):
        row = jnp.sum(jnp.where(place == b + 1, lab // CAP, 0), axis=0, keepdims=True)
        column = jnp.sum(jnp.where(square, row, 0), axis=1, keepdims=True)
        begin[b * CAP : (b + 1) * CAP, :] = jnp.broadcast_to(column.astype(F32), (CAP, HD))

    def unpacked(x):
        return jnp.dot(gather[...], x.reshape(slots, x.shape[2]), preferred_element_type=F32)

    kv_group().wait_recv()
    own = unpacked(kv_r[...])
    k_all[cx] = own[:, :HD].astype(BF16)
    v_all[cx] = jnp.transpose(own[:, HD:]).astype(BF16)

    def ctx_copies(n, block, there):
        return [
            pltpu.make_async_remote_copy(
                a.at[block], a.at[block], s.at[n], r.at[block],
                device_id=(me, there), device_id_type=MESH,
            )
            for a, s, r in ((k_all, k_ss, k_rs), (v_all, v_ss, v_rs))
        ]

    ups = [(n, n > y, n * 2 + low) for n in (3, 2, 1)]

    for a, s, r in ((k_all, k_ss, k_rs), (v_all, v_ss, v_rs)):
        step_rows = a.shape[1] // 4
        for i in range(4):
            piece = a.at[cx, pl.ds(i * step_rows, step_rows)]
            pltpu.make_async_remote_copy(
                piece, piece, s.at[0], r.at[cx], device_id=(me, mate), device_id_type=MESH
            ).start()

    def send_up(base, block):
        for part in (0, 1):
            for n, live, there in ups:

                @pl.when(live)
                def _(n=n, there=there, part=part):
                    ctx_copies(base + n, block, there)[part].start()

    send_up(0, cx)
    for c in ctx_copies(0, mate, mate):
        c.wait_recv()

    send_up(3, mate)
    for c in ctx_copies(0, cx, mate):
        c.wait_send()
    send_chunk(1)
    first = jnp.transpose(begin[...])[0:1, :].astype(I32)
    last = lax.broadcasted_iota(I32, (1, ROWS), 1) + cx * ROWS
    key_row = lax.broadcasted_iota(I32, (PAIR, ROWS), 0)

    def draw_mask(i, _):
        start = (y - i) * PAIR
        keep = (key_row >= first - start) & (key_row <= last - start)
        bias[i] = jnp.where(keep, 0.0, NEG)
        return 0

    lax.fori_loop(0, y + 1, draw_mask, 0)
    q_group(0).wait_send()
    send_chunk(2)
    ones = jnp.ones((SUMS - HD, PAIR), BF16)

    def attend(got, start, size, await_keys):
        width = size * ROWS
        mine = unpacked(got)
        for h in range(size):
            x = jnp.transpose(mine[:, h * HD : (h + 1) * HD])
            q_cols[:, h * ROWS : (h + 1) * ROWS] = x.astype(BF16)

        def await_pair(i, part):
            @pl.when(await_keys & (i > 0))
            def _():
                for block in (2 * (y - i), 2 * (y - i) + 1):
                    ctx_copies(0, block, mate)[part].wait_recv()

        def rate(i, k, top):
            keys = k.shape[0]
            s = jnp.dot(k, q_cols[:, :width], preferred_element_type=F32) * FACTOR
            s = s + jnp.concatenate([bias[i, :keys]] * size, axis=1)
            scores[i, :keys, :width] = s
            return jnp.maximum(top, jnp.max(s.reshape(keys // 8, 8, width), axis=0))

        def own_first(n, top):
            return rate(0, k_all[cx], top)

        def first_pass(i, top):
            pair = y - i
            await_pair(i, 0)
            k = jnp.concatenate([k_all[2 * pair], k_all[2 * pair + 1]], axis=0)
            return rate(i, k, top)

        top = jnp.full((8, width), NEG, F32)
        top = lax.fori_loop(0, 1 - low, own_first, top)
        top = lax.fori_loop(1 - low, y + 1, first_pass, top)
        peak = jnp.max(top, axis=0, keepdims=True)

        def add(i, v, total):
            keys = v.shape[1]
            w = jnp.exp2(scores[i, :keys, :width] - peak).astype(BF16)
            v = jnp.concatenate([v, ones[:, :keys]], axis=0)
            return total + jnp.dot(v, w, preferred_element_type=F32)

        def own_second(n, total):
            return add(0, v_all[cx], total)

        def second_pass(i, total):
            pair = y - i
            await_pair(i, 1)
            v = jnp.concatenate([v_all[2 * pair], v_all[2 * pair + 1]], axis=1)
            return add(i, v, total)

        total = jnp.zeros((SUMS, width), F32)
        total = lax.fori_loop(0, 1 - low, own_second, total)
        total = lax.fori_loop(1 - low, y + 1, second_pass, total)
        done = total[:HD] / total[HD : HD + 1]
        for h in range(size):
            at = pl.ds(pl.multiple_of((start + h) * HD, HD), HD)
            out[:, at] = jnp.transpose(done[:, h * ROWS : (h + 1) * ROWS]).astype(BF16)

    def double(ch, _):
        held, got = q_s2.at[ch], q_r2.at[ch]
        group(held.at[others], got.at[others], q_ss.at[ch], q_rs.at[ch]).wait_recv()

        @pl.when(ch == 1)
        def _():
            send_chunk(3)

        @pl.when(ch == 2)
        def _():
            send_chunk(4)

        attend(q_r2[ch], 2 * ch, 2, ch == 0)
        return 0

    def single(n, _):
        held, got = q_s1.at[n], q_r1.at[n]
        group(held.at[others], got.at[others], q_ss.at[n + 3], q_rs.at[n + 3]).wait_recv()
        attend(q_r1[n], n + 6, 1, n < 0)
        return 0

    lax.fori_loop(0, 3, double, 0)
    lax.fori_loop(0, 2, single, 0)

    labels.wait_send()
    for ch in range(1, CHUNKS):
        q_group(ch).wait_send()


    for n, live, there in ups:

        @pl.when(live)
        def _(n=n, there=there):
            for c in ctx_copies(n, cx, there):
                c.wait_send()
            for c in ctx_copies(3 + n, mate, there):
                c.wait_send()


def local(queries, keys_values, routing, documents):
    dma = pltpu.SemaphoreType.DMA
    anywhere = pl.BlockSpec(memory_space=pl.ANY)
    return pl.pallas_call(
        kernel,
        out_shape=pltpu.VMEM((ROWS, HEADS * HD), BF16),
        in_specs=[anywhere] * 4,
        out_specs=pl.BlockSpec(memory_space=pltpu.VMEM),
        scratch_shapes=[
            pltpu.VMEM((2, ROWS), I32),
            pltpu.VMEM((1, ROWS), I32),
            pltpu.VMEM((ROWS, HEADS * HD), BF16),
            pltpu.VMEM((ROWS, 2, HD), BF16),
            pltpu.VMEM((DP, 1, HD), I32),
            pltpu.VMEM((DP, 1, HD), I32),
            pltpu.VMEM((DP, CAP, 2 * HD), BF16),
            pltpu.VMEM((DP, CAP, 2 * HD), BF16),
            pltpu.VMEM((3, DP, CAP, 2 * HD), BF16),
            pltpu.VMEM((3, DP, CAP, 2 * HD), BF16),
            pltpu.VMEM((2, DP, CAP, HD), BF16),
            pltpu.VMEM((2, DP, CAP, HD), BF16),
            pltpu.VMEM((DP * CAP, ROWS), BF16),
            pltpu.VMEM((ROWS, DP * CAP), BF16),
            pltpu.VMEM((ROWS, HD), F32),
            pltpu.VMEM((CTX, ROWS, HD), BF16),
            pltpu.VMEM((CTX, HD, ROWS), BF16),
            pltpu.VMEM((HD, MOST * ROWS), BF16),
            pltpu.VMEM((CTX // 2, PAIR, ROWS), F32),
            pltpu.VMEM((CTX // 2, PAIR, MOST * ROWS), F32),
            dma((4,)), dma, dma, dma, dma, dma((CHUNKS,)), dma((CHUNKS,)),
            dma((7,)), dma((7,)), dma((CTX,)), dma((CTX,)),
        ],
        compiler_params=pltpu.CompilerParams(
            collective_id=1, has_side_effects=True, vmem_limit_bytes=56 << 20
        ),
        cost_estimate=pl.CostEstimate(
            flops=8 << 30, bytes_accessed=4 << 20, transcendentals=16 << 20
        ),
        name="relay_attend",
    )(routing.T, documents.reshape(1, ROWS), queries, keys_values.reshape(ROWS, 2, HD))


def solution(mesh):
    placed = (
        P(("dp", "ctx"), None),
        P(("dp", "ctx"), None, None, None),
        P(("dp", "ctx"), None),
        P(("dp", "ctx")),
    )
    return jax.shard_map(
        local, mesh=mesh, in_specs=placed, out_specs=P(("dp", "ctx"), None), check_vma=False
    )
```
